256 devices in a mesh: path: 8 (over z), tm: 32 (over x, y, core).
Axes of the slice: x: 4, y: 4, z: 8, core: 2. Of those that a mesh axis runs over, the one named last changes fastest.
Arguments:
- values: bfloat16 [4096, 64, 2048], P('path', 'tm'), may hold values from -5 to 5
- hazard: float32 [64, 4096], P('tm', 'path'), may hold values from 0.003125 to 0.046875
- spread: float32 [64], P('tm'), may hold values from 0.3 to 3
- trade_set: int32 [2048], replicated, may hold values from 0 to 255
Outputs:
- pathwise_fva: float32 [4096, 256], P(('path', 'tm'))
- set_fva: float32 [256], P(('path', 'tm'))
The draws below stay inside these ranges and needn't reach their ends.
All inputs are finite; a program needn't handle non-finite values.
Results may differ from the reference program's by a relative error of at most 0.0003.
Values sent between devices are 32-bit elements; how exact they have to be, the bound alone decides.
No kernel may reach another device: no remote copies, remote signals or barrier semaphores. Data moves between devices by JAX's collectives and lax.ppermute only.
A program may use at most 64 MiB of HBM per device.

```python
import math
import jax
import jax.numpy as jnp
from jax import lax

TRADES = 2048
SETS = 256
PATH_DEV = 512
PATHS = 4096
DATES = 64


def set_ends(result, rng, least, largest):
    extent = result.shape
    place = [jax.random.randint(jax.random.fold_in(rng, axis), (), 0, extent[axis]) for axis in range(len(extent))]
    result = result.at[tuple(place)].set(least)
    longest = extent.index(max(extent))
    place[longest] = (place[longest] + 1) % extent[longest]
    return result.at[tuple(place)].set(largest)


def block_levels(key, dims, shards, smallest, largest):
    gain, own = 1.0, jax.random.fold_in(key, 6)
    for axis_at, blocks in shards:
        draws = jnp.exp(jax.random.uniform(jax.random.fold_in(own, axis_at), (blocks,), jnp.float32, smallest / len(shards), largest / len(shards)))
        gain = gain * jnp.repeat(draws, dims[axis_at] // blocks).reshape([-1 if axis == axis_at else 1 for axis in range(len(dims))])
    return gain


def normal_values(own_key, shape, deviation, bound, shards=(), kind=jnp.bfloat16):
    result = jax.random.normal(own_key, shape, jnp.float32) * deviation
    if len(shards) > 0:
        result = block_levels(own_key, shape, shards, -0.22, 0.18) * result
    return jnp.clip(result, min=-bound, max=bound).astype(kind)


def setup_inputs(seed: int = 0) -> dict:
    keys = jax.random.split(jax.random.key(seed), 5)
    values = normal_values(keys[0], (PATHS, DATES, TRADES), 0.35, 5.0, ((0, 8), (1, 32)))
    hazard = jnp.clip(jnp.exp(math.log(0.046875) - 2.7080502 * jax.random.uniform(keys[1], (DATES, PATHS), jnp.float32) ** block_levels(keys[1], (DATES, PATHS), ((0, 32), (1, 8)), -0.2, 0.2)), 0.003125, 0.046875)
    spread = jnp.clip(jnp.exp(math.log(3.0) - 2.3025851 * jax.random.uniform(keys[2], (DATES,), jnp.float32) ** block_levels(keys[2], (DATES,), ((0, 32),), -0.2, 0.2)), 0.3, 3.0)
    trade_set = set_ends(jax.random.randint(keys[3], (TRADES,), 0, SETS), jax.random.fold_in(keys[3], 1), 0, SETS - 1).astype(jnp.int32)
    return dict(values=values, hazard=hazard, spread=spread, trade_set=trade_set)


def reference(values, hazard, spread, trade_set):
    onehot = (trade_set[:, None] == jnp.arange(SETS, dtype=jnp.int32)[None, :]).astype(jnp.bfloat16)
    survival = jnp.exp(-jnp.cumsum(hazard, axis=0))
    weights = spread[:, None] * survival
    blocks = PATHS // PATH_DEV
    value_blocks = values.reshape(blocks, PATH_DEV, DATES, TRADES)
    weight_blocks = jnp.transpose(weights.reshape(DATES, blocks, PATH_DEV), (1, 2, 0))

    def one_block(item):
        block_values, block_weights = item
        netted = jnp.dot(block_values.reshape(PATH_DEV * DATES, TRADES), onehot, preferred_element_type=jnp.float32)
        positive = jnp.maximum(netted.reshape(PATH_DEV, DATES, SETS), 0.0)
        return jnp.einsum("pt,pts->ps", block_weights, positive, precision=lax.Precision.HIGHEST)

    pathwise_fva = lax.map(one_block, (value_blocks, weight_blocks)).reshape(PATHS, SETS) / DATES
    set_fva = jnp.sum(pathwise_fva, axis=0) / PATHS
    return pathwise_fva, set_fva
```

```python
import jax
import jax.numpy as jnp
from jax import lax
from jax.experimental import pallas as pl
from jax.experimental.pallas import tpu as pltpu
from jax.sharding import Mesh
from jax.sharding import PartitionSpec as P

SETS = 256
LANES = 128
ROWS = 128
XY = 16
DATES = 64
PATHS = 4096
MIB = 2**20
VMEM = pl.BlockSpec(memory_space=pltpu.VMEM)
SMEM = pl.BlockSpec(memory_space=pltpu.SMEM)
HALF = jax.ShapeDtypeStruct((XY, 32, LANES), jnp.float32)
SET_ROWS = jax.ShapeDtypeStruct((XY, 2, LANES), jnp.float32)


def columns(row):
    return jnp.transpose(jnp.broadcast_to(row, (LANES, LANES)))


def hazard_kernel(hazard_ref, out_ref):
    own = hazard_ref[0:1, :] + hazard_ref[1:2, :]
    for part in range(4):
        lanes = slice(part * LANES, (part + 1) * LANES)
        out_ref[:, part, :] = jnp.broadcast_to(own[:, lanes], (32, LANES))


def hazard_sums(hazard):
    return pl.pallas_call(
        hazard_kernel,
        out_shape=jax.ShapeDtypeStruct((32, 4, LANES), jnp.float32),
        in_specs=[VMEM],
        out_specs=VMEM,
        compiler_params=pltpu.CompilerParams(vmem_limit_bytes=2 * MIB),
        cost_estimate=pl.CostEstimate(flops=5 * 10**9, bytes_accessed=2**16, transcendentals=0),
        name="hazard_sums",
    )(hazard)


def net_kernel(values_ref, hazard_ref, spread_ref, set_ref, both_ref, net_ref):
    ids = lax.broadcasted_iota(jnp.int32, (SETS, set_ref.shape[1]), 0)
    onehot = jnp.where(ids == set_ref[...], 1.0, 0.0).astype(jnp.bfloat16)
    first = hazard_ref[0:1, :]
    weight_0 = spread_ref[0] * jnp.exp(-first)
    weight_1 = spread_ref[1] * jnp.exp(-(first + hazard_ref[1:2, :]))
    for at in range(0, values_ref.shape[0], ROWS):
        block = values_ref[at : at + ROWS].reshape(2 * ROWS, values_ref.shape[2])
        netted = lax.dot_general(
            block, onehot, (((1,), (1,)), ((), ())), preferred_element_type=jnp.float32
        )
        column_0 = columns(weight_0[:, at : at + ROWS])
        column_1 = columns(weight_1[:, at : at + ROWS])
        for half in range(2):
            lanes = slice(half * LANES, (half + 1) * LANES)
            net_ref[half, 2 * at : 2 * at + 2 * ROWS] = netted[:, lanes]
            even = net_ref[half, pl.ds(2 * at, ROWS, 2), :]
            odd = net_ref[half, pl.ds(2 * at + 1, ROWS, 2), :]
            funded = column_0 * jnp.maximum(even, 0.0) + column_1 * jnp.maximum(odd, 0.0)
            for j in range(ROWS // 16):
                block_at = at // 16 + j
                both_ref[block_at % 2, block_at // 2, half * 16 : half * 16 + 16, :] = funded[
                    j * 16 : j * 16 + 16, :
                ]


def local_sums(values, hazard, spread, trade_set):
    paths, dates, trades = values.shape
    return pl.pallas_call(
        net_kernel,
        out_shape=jax.ShapeDtypeStruct((2, XY, 32, LANES), jnp.float32),
        in_specs=[VMEM, VMEM, SMEM, VMEM],
        out_specs=VMEM,
        scratch_shapes=[pltpu.VMEM((2, paths * dates, LANES), jnp.float32)],
        compiler_params=pltpu.CompilerParams(vmem_limit_bytes=20 * MIB),
        cost_estimate=pl.CostEstimate(
            flops=2 * paths * dates * trades * SETS, bytes_accessed=5 * MIB, transcendentals=1024
        ),
        name="local_sums",
    )(values, hazard, spread, trade_set[None, :])


def scale_kernel(gathered_ref, sums_ref, keep_ref, give_ref, parts_ref, column_ref):
    core = lax.axis_index("c")
    me = (lax.axis_index("x") * 4 + lax.axis_index("y")) * 2 + core
    block = lax.broadcasted_iota(jnp.int32, gathered_ref.shape, 0)
    prefix = jnp.sum(jnp.where(block < me, gathered_ref[...], 0.0), axis=0)
    earlier = jnp.exp(-prefix) * (1.0 / DATES)
    for part in range(4):
        column_ref[part * ROWS : (part + 1) * ROWS, :] = columns(earlier[part : part + 1, :])
    total = [jnp.zeros((16, LANES), jnp.float32)] * 2
    for parity, out_ref in ((core, keep_ref), (1 - core, give_ref)):
        for i in range(XY):
            column = column_ref[pl.ds(pl.multiple_of((2 * i + parity) * 16, 16), 16), :]
            for half in range(2):
                at = slice(half * 16, half * 16 + 16)
                scaled = column * sums_ref[parity, i, at, :]
                out_ref[i, at, :] = scaled
                total[half] = total[half] + scaled
    for half in range(2):
        row = jnp.sum(total[half], axis=0, keepdims=True) * (1.0 / PATHS)
        parts_ref[:, half, :] = jnp.broadcast_to(row, (XY, LANES))


def scaled_sums(gathered, sums):
    return pl.pallas_call(
        scale_kernel,
        out_shape=(HALF, HALF, SET_ROWS),
        in_specs=[VMEM, VMEM],
        out_specs=(VMEM, VMEM, VMEM),
        scratch_shapes=[pltpu.VMEM((4 * ROWS, LANES), jnp.float32)],
        compiler_params=pltpu.CompilerParams(vmem_limit_bytes=4 * MIB),
        cost_estimate=pl.CostEstimate(flops=10**6, bytes_accessed=MIB, transcendentals=1024),
        name="scaled_sums",
    )(gathered, sums)


def join_kernel(keep_ref, got_ref, parts_ref, out_ref):
    out_ref[:, 0:32, :] = keep_ref[...] + got_ref[...]
    total = jnp.sum(parts_ref[...], axis=0)
    for half in range(2):
        row = jnp.broadcast_to(total[half : half + 1, :], (4, LANES))
        for i in range(XY):
            out_ref[i, 32 + half * 4 : 36 + half * 4, :] = row


def joined(keep, got, parts):
    return pl.pallas_call(
        join_kernel,
        out_shape=jax.ShapeDtypeStruct((XY, 40, LANES), jnp.float32),
        in_specs=[VMEM, VMEM, VMEM],
        out_specs=VMEM,
        compiler_params=pltpu.CompilerParams(vmem_limit_bytes=4 * MIB),
        cost_estimate=pl.CostEstimate(flops=10**5, bytes_accessed=MIB, transcendentals=0),
        name="joined",
    )(keep, got, parts)


def last_kernel(arrived_ref, paths_ref, set_ref):
    total = jnp.sum(arrived_ref[...], axis=0)
    for half in range(2):
        paths_ref[:, half * LANES : (half + 1) * LANES] = total[half * 16 : half * 16 + 16, :]
    tm = (lax.axis_index("x") * 4 + lax.axis_index("y")) * 2 + lax.axis_index("c")
    me = lax.axis_index("z") * 32 + tm
    row = lax.broadcasted_iota(jnp.int32, (8, LANES), 0)
    lane = lax.broadcasted_iota(jnp.int32, (8, LANES), 1)
    mine = (row == me // LANES * 4) & (lane == me % LANES)
    own = jnp.sum(jnp.where(mine, total[32:40, :], 0.0), axis=(0, 1), keepdims=True)
    set_ref[...] = jnp.broadcast_to(own, (1, LANES))


def last_sums(arrived):
    return pl.pallas_call(
        last_kernel,
        out_shape=(
            jax.ShapeDtypeStruct((16, SETS), jnp.float32),
            jax.ShapeDtypeStruct((1, LANES), jnp.float32),
        ),
        in_specs=[VMEM],
        out_specs=(VMEM, VMEM),
        compiler_params=pltpu.CompilerParams(vmem_limit_bytes=4 * MIB),
        name="last_sums",
    )(arrived)


def on_device(values, hazard, spread, trade_set):
    gathered = lax.all_to_all(hazard_sums(hazard), ("x", "y", "c"), 0, 0, tiled=True)
    sums = local_sums(values, hazard, spread, trade_set)
    keep, give, parts = scaled_sums(gathered, sums)
    parts = lax.all_to_all(parts, ("z", "c"), 0, 0, tiled=True)
    got = lax.ppermute(give, "c", [(0, 1), (1, 0)])
    arrived = lax.all_to_all(joined(keep, got, parts), ("x", "y"), 0, 0, tiled=True)
    pathwise, sets = last_sums(arrived)
    return pathwise, sets[0, 0:1]


def solution(mesh):
    split = Mesh(mesh.devices.reshape(mesh.shape["path"], 4, 4, 2), ("z", "x", "y", "c"))
    tm = ("x", "y", "c")
    every = ("z", "x", "y", "c")
    return jax.shard_map(
        on_device,
        mesh=split,
        in_specs=(P("z", tm, None), P(tm, "z"), P(tm), P()),
        out_specs=(P(every, None), P(every)),
        check_vma=False,
    )
```

```python
import jax
import jax.numpy as jnp
from jax import lax
from jax.experimental import pallas as pl
from jax.experimental.pallas import tpu as pltpu
from jax.sharding import Mesh
from jax.sharding import PartitionSpec as P

SETS = 256
LANES = 128
ROWS = 128
XY = 16
DATES = 64
PATHS = 4096
MIB = 2**20
VMEM = pl.BlockSpec(memory_space=pltpu.VMEM)
SMEM = pl.BlockSpec(memory_space=pltpu.SMEM)
HALF = jax.ShapeDtypeStruct((XY, 32, LANES), jnp.float32)
SET_ROWS = jax.ShapeDtypeStruct((XY, 2, LANES), jnp.float32)


def columns(row):
    return jnp.transpose(jnp.broadcast_to(row, (LANES, LANES)))


def hazard_kernel(hazard_ref, out_ref):
    own = hazard_ref[0:1, :] + hazard_ref[1:2, :]
    for part in range(4):
        lanes = slice(part * LANES, (part + 1) * LANES)
        out_ref[:, part, :] = jnp.broadcast_to(own[:, lanes], (32, LANES))


def hazard_sums(hazard):
    return pl.pallas_call(
        hazard_kernel,
        out_shape=jax.ShapeDtypeStruct((32, 4, LANES), jnp.float32),
        in_specs=[VMEM],
        out_specs=VMEM,
        compiler_params=pltpu.CompilerParams(vmem_limit_bytes=2 * MIB),
        cost_estimate=pl.CostEstimate(flops=5 * 10**9, bytes_accessed=2**16, transcendentals=0),
        name="hazard_sums",
    )(hazard)


def net_kernel(hbm_ref, hazard_ref, spread_ref, set_ref, both_ref, values_ref, net_ref, hot_ref, sem):
    copies = []
    for at in range(0, hbm_ref.shape[0], 256):
        block = pl.ds(at, 256)
        copies.append(
            pltpu.make_async_copy(hbm_ref.at[block], values_ref.at[block], sem.at[at // 256])
        )
        copies[-1].start()
    lane = lax.broadcasted_iota(jnp.int32, (LANES, LANES), 1)
    for at in range(0, set_ref.shape[1], LANES):
        ids = columns(set_ref[:, at : at + LANES])
        for half in range(2):
            hot_ref[at : at + LANES, half * LANES : (half + 1) * LANES] = jnp.where(
                ids == lane + half * LANES, 1.0, 0.0
            ).astype(jnp.bfloat16)
    first = hazard_ref[0:1, :]
    weight_0 = spread_ref[0] * jnp.exp(-first)
    weight_1 = spread_ref[1] * jnp.exp(-(first + hazard_ref[1:2, :]))
    for at in range(0, values_ref.shape[0], ROWS):
        if at == 0:
            copies[0].wait()
        if at == 256:
            copies[1].wait()
        block = values_ref[at : at + ROWS].reshape(2 * ROWS, values_ref.shape[2])
        netted = lax.dot_general(
            block, hot_ref[...], (((1,), (0,)), ((), ())), preferred_element_type=jnp.float32
        )
        column_0 = columns(weight_0[:, at : at + ROWS])
        column_1 = columns(weight_1[:, at : at + ROWS])
        for half in range(2):
            lanes = slice(half * LANES, (half + 1) * LANES)
            net_ref[half, 2 * at : 2 * at + 2 * ROWS] = netted[:, lanes]
            even = net_ref[half, pl.ds(2 * at, ROWS, 2), :]
            odd = net_ref[half, pl.ds(2 * at + 1, ROWS, 2), :]
            funded = column_0 * jnp.maximum(even, 0.0) + column_1 * jnp.maximum(odd, 0.0)
            for j in range(ROWS // 16):
                block_at = at // 16 + j
                both_ref[block_at % 2, block_at // 2, pl.ds(half, 16, 2), :] = funded[
                    j * 16 : j * 16 + 16, :
                ]


def local_sums(values, hazard, spread, trade_set):
    paths, dates, trades = values.shape
    return pl.pallas_call(
        net_kernel,
        out_shape=jax.ShapeDtypeStruct((2, XY, 32, LANES), jnp.float32),
        in_specs=[pl.BlockSpec(memory_space=pl.ANY), VMEM, SMEM, VMEM],
        out_specs=VMEM,
        scratch_shapes=[
            pltpu.VMEM(values.shape, values.dtype),
            pltpu.VMEM((2, paths * dates, LANES), jnp.float32),
            pltpu.VMEM((trades, SETS), jnp.bfloat16),
            pltpu.SemaphoreType.DMA((paths // 256,)),
        ],
        compiler_params=pltpu.CompilerParams(vmem_limit_bytes=12 * MIB),
        cost_estimate=pl.CostEstimate(
            flops=2 * paths * dates * trades * SETS, bytes_accessed=5 * MIB, transcendentals=1024
        ),
        name="local_sums",
    )(pltpu.with_memory_space_constraint(values, pltpu.HBM), hazard, spread, trade_set[None, :])


def row_kernel(gathered_ref, sums_ref, column_ref, parts_ref, total_ref):
    core = lax.axis_index("c")
    me = (lax.axis_index("x") * 4 + lax.axis_index("y")) * 2 + core
    block = lax.broadcasted_iota(jnp.int32, gathered_ref.shape, 0)
    prefix = jnp.sum(jnp.where(block < me, gathered_ref[...], 0.0), axis=0)
    earlier = jnp.exp(-prefix) * (1.0 / DATES)
    for part in range(4):
        column = columns(earlier[part : part + 1, :])
        for half in range(2):
            column_ref[pl.ds(2 * part * ROWS + half, ROWS, 2), :] = column
    total = jnp.zeros((32, LANES), jnp.float32)
    for i in range(XY):
        for parity in range(2):
            rows = slice((2 * i + parity) * 32, (2 * i + parity + 1) * 32)
            total = total + column_ref[rows, :] * sums_ref[parity, i]
    total_ref[...] = total
    for half in range(2):
        row = jnp.sum(total_ref[pl.ds(half, 16, 2), :], axis=0, keepdims=True) * (1.0 / PATHS)
        parts_ref[:, half, :] = jnp.broadcast_to(row, (XY, LANES))


def set_rows(gathered, sums):
    return pl.pallas_call(
        row_kernel,
        out_shape=(jax.ShapeDtypeStruct((8 * ROWS, LANES), jnp.float32), SET_ROWS),
        in_specs=[VMEM, VMEM],
        out_specs=(VMEM, VMEM),
        scratch_shapes=[pltpu.VMEM((32, LANES), jnp.float32)],
        compiler_params=pltpu.CompilerParams(vmem_limit_bytes=4 * MIB),
        cost_estimate=pl.CostEstimate(flops=10**6, bytes_accessed=MIB, transcendentals=1024),
        name="set_rows",
    )(gathered, sums)


def scale_kernel(column_ref, sums_ref, keep_ref, give_ref):
    core = lax.axis_index("c")
    for parity, out_ref in ((core, keep_ref), (1 - core, give_ref)):
        for i in range(XY):
            rows = pl.ds(pl.multiple_of((2 * i + parity) * 32, 32), 32)
            out_ref[i] = column_ref[rows, :] * sums_ref[parity, i]


def scaled_sums(column, sums):
    return pl.pallas_call(
        scale_kernel,
        out_shape=(HALF, HALF),
        in_specs=[VMEM, VMEM],
        out_specs=(VMEM, VMEM),
        compiler_params=pltpu.CompilerParams(vmem_limit_bytes=4 * MIB),
        cost_estimate=pl.CostEstimate(flops=10**6, bytes_accessed=MIB, transcendentals=0),
        name="scaled_sums",
    )(column, sums)


def join_kernel(keep_ref, got_ref, parts_ref, out_ref):
    total = jnp.sum(parts_ref[...], axis=0)
    rows_ref = out_ref.reshape(XY * 34, LANES)
    for i in range(XY):
        rows_ref[i * 34 : i * 34 + 32, :] = keep_ref[i] + got_ref[i]
        rows_ref[i * 34 + 32 : i * 34 + 34, :] = total


def joined(keep, got, parts):
    return pl.pallas_call(
        join_kernel,
        out_shape=jax.ShapeDtypeStruct((XY, 17, 2, LANES), jnp.float32),
        in_specs=[VMEM, VMEM, VMEM],
        out_specs=VMEM,
        compiler_params=pltpu.CompilerParams(vmem_limit_bytes=4 * MIB),
        cost_estimate=pl.CostEstimate(flops=10**5, bytes_accessed=MIB, transcendentals=0),
        name="joined",
    )(keep, got, parts)


def last_kernel(arrived_ref, paths_ref, set_ref, total_ref):
    rows_ref = arrived_ref.reshape(XY * 34, LANES)
    total = rows_ref[0:34, :]
    for i in range(1, XY):
        total = total + rows_ref[i * 34 : i * 34 + 34, :]
    total_ref[0:34, :] = total
    for half in range(2):
        paths_ref[:, half * LANES : (half + 1) * LANES] = total_ref[pl.ds(half, 16, 2), :]
    tm = (lax.axis_index("x") * 4 + lax.axis_index("y")) * 2 + lax.axis_index("c")
    me = lax.axis_index("z") * 32 + tm
    row = lax.broadcasted_iota(jnp.int32, (2, LANES), 0)
    lane = lax.broadcasted_iota(jnp.int32, (2, LANES), 1)
    mine = row * LANES + lane == me
    own = jnp.sum(jnp.where(mine, total_ref[32:34, :], 0.0), axis=(0, 1), keepdims=True)
    set_ref[...] = jnp.broadcast_to(own, (1, LANES))


def last_sums(arrived):
    return pl.pallas_call(
        last_kernel,
        out_shape=(
            jax.ShapeDtypeStruct((16, SETS), jnp.float32),
            jax.ShapeDtypeStruct((1, LANES), jnp.float32),
        ),
        in_specs=[VMEM],
        out_specs=(VMEM, VMEM),
        scratch_shapes=[pltpu.VMEM((40, LANES), jnp.float32)],
        compiler_params=pltpu.CompilerParams(vmem_limit_bytes=4 * MIB),
        name="last_sums",
    )(arrived)


def on_device(values, hazard, spread, trade_set):
    gathered = lax.all_to_all(hazard_sums(hazard), ("x", "y", "c"), 0, 0, tiled=True)
    sums = local_sums(values, hazard, spread, trade_set)
    column, parts = set_rows(gathered, sums)
    keep, give = scaled_sums(column, sums)
    parts = lax.all_to_all(parts, ("z", "c"), 0, 0, tiled=True)
    got = lax.ppermute(give, "c", [(0, 1), (1, 0)])
    arrived = lax.all_to_all(joined(keep, got, parts), ("x", "y"), 0, 0, tiled=True)
    pathwise, sets = last_sums(arrived)
    return pathwise, sets[0, 0:1]


def solution(mesh):
    split = Mesh(mesh.devices.reshape(mesh.shape["path"], 4, 4, 2), ("z", "x", "y", "c"))
    tm = ("x", "y", "c")
    every = ("z", "x", "y", "c")
    return jax.shard_map(
        on_device,
        mesh=split,
        in_specs=(P("z", tm, None), P(tm, "z"), P(tm), P()),
        out_specs=(P(every, None), P(every)),
        check_vma=False,
    )
```

```python
import jax
import jax.numpy as jnp
from jax import lax
from jax.experimental import pallas as pl
from jax.experimental.pallas import tpu as pltpu
from jax.sharding import Mesh
from jax.sharding import PartitionSpec as P

SETS = 256
LANES = 128
ROWS = 128
XY = 16
DATES = 64
PATHS = 4096
MESSAGE = 66
MIB = 2**20
VMEM = pl.BlockSpec(memory_space=pltpu.VMEM)
ANY = pl.BlockSpec(memory_space=pl.ANY)
HALF_ROWS = XY * 32
HALF = jax.ShapeDtypeStruct((HALF_ROWS + 8, LANES), jnp.float32)


def columns(row):
    return jnp.transpose(jnp.broadcast_to(row, (LANES, LANES)))


def in_hbm(array):
    return pltpu.with_memory_space_constraint(array, pltpu.HBM)


def net_kernel(
    values_hbm,
    hazard_hbm,
    spread_hbm,
    set_hbm,
    keep_ref,
    give_ref,
    values_ref,
    hazard_ref,
    spread_ref,
    set_ref,
    net_ref,
    hot_ref,
    both_ref,
    sem,
):
    half_paths = values_hbm.shape[0] // 2
    small = [
        pltpu.make_async_copy(set_hbm, set_ref, sem.at[0]),
        pltpu.make_async_copy(hazard_hbm, hazard_ref, sem.at[1]),
        pltpu.make_async_copy(spread_hbm, spread_ref, sem.at[2]),
    ]
    large = [
        pltpu.make_async_copy(
            values_hbm.at[pl.ds(part * half_paths, half_paths)],
            values_ref.at[pl.ds(part * half_paths, half_paths)],
            sem.at[3 + part],
        )
        for part in range(2)
    ]
    for copy in small + large:
        copy.start()
    for copy in small:
        copy.wait()
    lane = lax.broadcasted_iota(jnp.int32, (LANES, LANES), 1)
    for at in range(0, set_ref.shape[1], LANES):
        ids = columns(set_ref[:, at : at + LANES])
        for half in range(2):
            hot_ref[at : at + LANES, half * LANES : (half + 1) * LANES] = jnp.where(
                ids == lane + half * LANES, 1.0, 0.0
            ).astype(jnp.bfloat16)
    first = hazard_ref[0:1, :]
    weight_0 = spread_ref[:, 0:1] * jnp.exp(-first)
    weight_1 = spread_ref[:, 1:2] * jnp.exp(-(first + hazard_ref[1:2, :]))
    for at in range(0, values_ref.shape[0], ROWS):
        if at % half_paths == 0:
            large[at // half_paths].wait()
        block = values_ref[at : at + ROWS].reshape(2 * ROWS, values_ref.shape[2])
        netted = jnp.dot(block, hot_ref[...], preferred_element_type=jnp.float32)
        column_0 = columns(weight_0[:, at : at + ROWS])
        column_1 = columns(weight_1[:, at : at + ROWS])
        for half in range(2):
            net_ref[half, 2 * at : 2 * at + 2 * ROWS] = netted[
                :, half * LANES : (half + 1) * LANES
            ]
            even = net_ref[half, pl.ds(2 * at, ROWS, 2), :]
            odd = net_ref[half, pl.ds(2 * at + 1, ROWS, 2), :]
            funded = column_0 * jnp.maximum(even, 0.0) + column_1 * jnp.maximum(odd, 0.0)
            for j in range(ROWS // 16):
                block_at = at // 16 + j
                row_at = block_at // 2 * 32 + half * 16
                both_ref[block_at % 2, row_at : row_at + 16, :] = funded[j * 16 : j * 16 + 16, :]
    core = lax.axis_index("c")
    own = first + hazard_ref[1:2, :]
    own = [own[:, at : at + LANES] for at in range(0, own.shape[1], LANES)]
    own = jnp.concatenate(own + [jnp.zeros((4, LANES), jnp.float32)], axis=0)
    for out_ref, parity in ((keep_ref, core), (give_ref, 1 - core)):
        out_ref[0:HALF_ROWS, :] = both_ref[parity]
        out_ref[HALF_ROWS : HALF_ROWS + 8, :] = own


def local_sums(values, hazard, spread, trade_set):
    paths, dates, trades = values.shape
    return pl.pallas_call(
        net_kernel,
        out_shape=(HALF, HALF),
        in_specs=[ANY, ANY, ANY, ANY],
        out_specs=(VMEM, VMEM),
        scratch_shapes=[
            pltpu.VMEM(values.shape, values.dtype),
            pltpu.VMEM(hazard.shape, hazard.dtype),
            pltpu.VMEM((1, dates), jnp.float32),
            pltpu.VMEM((1, trades), jnp.int32),
            pltpu.VMEM((2, paths * dates, LANES), jnp.float32),
            pltpu.VMEM((trades, SETS), jnp.bfloat16),
            pltpu.VMEM((2, HALF_ROWS, LANES), jnp.float32),
            pltpu.SemaphoreType.DMA((5,)),
        ],
        compiler_params=pltpu.CompilerParams(vmem_limit_bytes=16 * MIB),
        cost_estimate=pl.CostEstimate(
            flops=2 * paths * dates * trades * SETS, bytes_accessed=5 * MIB, transcendentals=1024
        ),
        name="local_sums",
    )(in_hbm(values), in_hbm(hazard), in_hbm(spread[None, :]), in_hbm(trade_set[None, :]))


def pack_kernel(keep_ref, got_ref, out_ref, first_ref, sum_ref, kept_ref, turned_ref):
    rows_ref = out_ref.reshape(XY * MESSAGE, LANES)
    core = lax.axis_index("c")
    own = keep_ref[HALF_ROWS : HALF_ROWS + 4, :]
    other = got_ref[HALF_ROWS : HALF_ROWS + 4, :]
    early = jnp.exp(-jnp.where(core == 0, own, other))
    chip = own + other
    for part in range(4):
        rows = slice(part * ROWS, (part + 1) * ROWS)
        first_ref[rows, :] = columns(early[part : part + 1, :])
        sum_ref[rows, :] = columns(chip[part : part + 1, :])
    for part in range(2):
        halves = [[], []]
        for i in range(part * 8, part * 8 + 8):
            kept = pl.ds(pl.multiple_of((2 * i + core) * 16, 16), 16)
            factor = first_ref[kept, :]
            mine = jnp.where(core == 0, 1.0, factor)
            theirs = jnp.where(core == 0, factor, 1.0)
            kept_ref[i * 16 : i * 16 + 16, :] = sum_ref[kept, :]
            for half in range(2):
                rows = slice(i * 32 + half * 16, i * 32 + half * 16 + 16)
                both = mine * keep_ref[rows, :] + theirs * got_ref[rows, :]
                rows_ref[i * MESSAGE + half * 16 : i * MESSAGE + half * 16 + 16, :] = both
                halves[half].append(both)
        for half in range(2):
            turned_ref[part, half * LANES : (half + 1) * LANES, :] = jnp.transpose(
                jnp.concatenate(halves[half], axis=0)
            )
        sums = jnp.transpose(kept_ref[part * LANES : (part + 1) * LANES, :])[0:1, :]
        for i in range(XY):
            rows_ref[i * MESSAGE + 64 + part : i * MESSAGE + 65 + part, :] = sums
            for owner in range(2):
                at = i * MESSAGE + 32 + part * 16 + owner * 8
                rows_ref[at : at + 8, :] = turned_ref[part, pl.ds(2 * i + owner, 8, 32), :]


def packed(keep, got):
    return pl.pallas_call(
        pack_kernel,
        out_shape=jax.ShapeDtypeStruct((XY, MESSAGE // 2, 2, LANES), jnp.float32),
        in_specs=[VMEM, VMEM],
        out_specs=VMEM,
        scratch_shapes=[
            pltpu.VMEM((4 * ROWS, LANES), jnp.float32),
            pltpu.VMEM((4 * ROWS, LANES), jnp.float32),
            pltpu.VMEM((2 * ROWS, LANES), jnp.float32),
            pltpu.VMEM((2, SETS, LANES), jnp.float32),
        ],
        compiler_params=pltpu.CompilerParams(vmem_limit_bytes=4 * MIB),
        cost_estimate=pl.CostEstimate(flops=10**6, bytes_accessed=MIB, transcendentals=512),
        name="packed",
    )(keep, got)


def set_kernel(arrived_ref, earlier_ref, parts_ref):
    rows_ref = arrived_ref.reshape(XY * MESSAGE, LANES)
    prefix = jnp.zeros((2, LANES), jnp.float32)
    total = [jnp.zeros((16, LANES), jnp.float32)] * 2
    for k in range(XY):
        earlier = jnp.exp(-prefix) * (1.0 / DATES)
        for part in range(2):
            row = earlier[part : part + 1, :]
            earlier_ref[part, k : k + 1, :] = row
            at = k * MESSAGE + 32 + part * 16
            total[part] = total[part] + row * rows_ref[at : at + 16, :]
        prefix = prefix + rows_ref[k * MESSAGE + 64 : k * MESSAGE + 66, :]
    sums = jnp.sum(total[0] + total[1], axis=1, keepdims=True) * (1.0 / PATHS)
    parts_ref[...] = jnp.broadcast_to(sums, (16, LANES))[:, None, :]


def set_parts(arrived):
    return pl.pallas_call(
        set_kernel,
        out_shape=(
            jax.ShapeDtypeStruct((2, XY, LANES), jnp.float32),
            jax.ShapeDtypeStruct((16, 1, LANES), jnp.float32),
        ),
        in_specs=[VMEM],
        out_specs=(VMEM, VMEM),
        compiler_params=pltpu.CompilerParams(vmem_limit_bytes=2 * MIB),
        cost_estimate=pl.CostEstimate(flops=10**6, bytes_accessed=2**19, transcendentals=4096),
        name="set_parts",
    )(arrived)


def last_kernel(arrived_ref, earlier_ref, parts_ref, paths_ref, set_ref, turned_ref):
    rows_ref = arrived_ref.reshape(XY * MESSAGE, LANES)
    chip = lax.axis_index("x") * 4 + lax.axis_index("y")
    padding = jnp.zeros((LANES - XY, LANES), jnp.float32)
    for part in range(2):
        turned_ref[part * LANES : (part + 1) * LANES, :] = jnp.transpose(
            jnp.concatenate([earlier_ref[part], padding], axis=0)
        )
    own = turned_ref[pl.ds(pl.multiple_of(chip * 16, 16), 16), :]
    total = [jnp.zeros((16, LANES), jnp.float32)] * 2
    for k in range(XY):
        weight = own[:, k : k + 1]
        for half in range(2):
            at = k * MESSAGE + half * 16
            total[half] = total[half] + weight * rows_ref[at : at + 16, :]
    for half in range(2):
        paths_ref[:, half * LANES : (half + 1) * LANES] = total[half]
    set_ref[...] = jnp.sum(parts_ref[...], axis=0)


def last_sums(arrived, earlier, parts):
    return pl.pallas_call(
        last_kernel,
        out_shape=(
            jax.ShapeDtypeStruct((16, SETS), jnp.float32),
            jax.ShapeDtypeStruct((1, LANES), jnp.float32),
        ),
        in_specs=[VMEM, VMEM, VMEM],
        out_specs=(VMEM, VMEM),
        scratch_shapes=[pltpu.VMEM((2 * LANES, LANES), jnp.float32)],
        compiler_params=pltpu.CompilerParams(vmem_limit_bytes=2 * MIB),
        cost_estimate=pl.CostEstimate(flops=10**6, bytes_accessed=2**19, transcendentals=0),
        name="last_sums",
    )(arrived, earlier, parts)


def on_device(values, hazard, spread, trade_set):
    keep, give = local_sums(values, hazard, spread, trade_set)
    got = lax.ppermute(give, "c", [(0, 1), (1, 0)])
    arrived = lax.all_to_all(packed(keep, got), ("x", "y"), 0, 0, tiled=True)
    earlier, parts = set_parts(arrived)
    parts = lax.all_to_all(parts, ("c", "z"), 0, 0, tiled=True)
    pathwise, sets = last_sums(arrived, earlier, parts)
    return pathwise, sets[0, 0:1]


def solution(mesh):
    split = Mesh(mesh.devices.reshape(mesh.shape["path"], 4, 4, 2), ("z", "x", "y", "c"))
    tm = ("x", "y", "c")
    every = ("z", "x", "y", "c")
    return jax.shard_map(
        on_device,
        mesh=split,
        in_specs=(P("z", tm, None), P(tm, "z"), P(tm), P()),
        out_specs=(P(every, None), P(every)),
        check_vma=False,
    )
```

```python
import jax
import jax.numpy as jnp
from jax import lax
from jax.experimental import pallas as pl
from jax.experimental.pallas import tpu as pltpu
from jax.sharding import Mesh
from jax.sharding import PartitionSpec as P

SETS = 256
LANES = 128
ROWS = 128
XY = 16
DATES = 64
PATHS = 4096
MESSAGE = 68
MIB = 2**20
VMEM = pl.BlockSpec(memory_space=pltpu.VMEM)
ANY = pl.BlockSpec(memory_space=pl.ANY)
HALF_ROWS = XY * 32
HALF = jax.ShapeDtypeStruct((HALF_ROWS + 8, LANES), jnp.float32)


def columns(row):
    return jnp.transpose(jnp.broadcast_to(row, (LANES, LANES)))


def in_hbm(array):
    return pltpu.with_memory_space_constraint(array, pltpu.HBM)


def net_kernel(
    values_hbm,
    hazard_hbm,
    spread_hbm,
    set_hbm,
    keep_ref,
    give_ref,
    values_ref,
    hazard_ref,
    spread_ref,
    set_ref,
    net_ref,
    hot_ref,
    both_ref,
    own_ref,
    sem,
):
    half_paths = values_hbm.shape[0] // 2
    small = [
        pltpu.make_async_copy(set_hbm, set_ref, sem.at[0]),
        pltpu.make_async_copy(hazard_hbm, hazard_ref, sem.at[1]),
        pltpu.make_async_copy(spread_hbm, spread_ref, sem.at[2]),
    ]
    large = [
        pltpu.make_async_copy(
            values_hbm.at[pl.ds(part * half_paths, half_paths)],
            values_ref.at[pl.ds(part * half_paths, half_paths)],
            sem.at[3 + part],
        )
        for part in range(2)
    ]
    for copy in small + large:
        copy.start()
    for copy in small:
        copy.wait()
    lane = lax.broadcasted_iota(jnp.int32, (LANES, LANES), 1)
    for at in range(0, set_ref.shape[1], LANES):
        ids = columns(set_ref[:, at : at + LANES])
        for half in range(2):
            hot_ref[at : at + LANES, half * LANES : (half + 1) * LANES] = jnp.where(
                ids == lane + half * LANES, 1.0, 0.0
            ).astype(jnp.bfloat16)
    core = lax.axis_index("c")
    own = hazard_ref[0:1, :] + hazard_ref[1:2, :]
    before = jnp.where(core == 0, 0.0, own)
    weight_0 = spread_ref[:, 0:1] * jnp.exp(hazard_ref[1:2, :] - before)
    weight_1 = jnp.broadcast_to(spread_ref[:, 1:2], own.shape) * jnp.exp(-before)
    for at in range(0, own.shape[1], LANES):
        own_ref[at : at + LANES, :] = columns(own[:, at : at + LANES])
    for out_ref, parity in ((keep_ref, core), (give_ref, 1 - core)):
        for part in range(2):
            kept = [
                own_ref[pl.ds(pl.multiple_of((2 * i + parity) * 16, 16), 16), :]
                for i in range(part * 8, part * 8 + 8)
            ]
            row = jnp.transpose(jnp.concatenate(kept, axis=0))[0:1, :]
            out_ref[HALF_ROWS + part * 4 : HALF_ROWS + part * 4 + 4, :] = jnp.broadcast_to(
                row, (4, LANES)
            )
    for at in range(0, values_ref.shape[0], ROWS):
        if at % half_paths == 0:
            large[at // half_paths].wait()
        block = values_ref[at : at + ROWS].reshape(2 * ROWS, values_ref.shape[2])
        netted = jnp.dot(block, hot_ref[...], preferred_element_type=jnp.float32)
        column_0 = columns(weight_0[:, at : at + ROWS])
        column_1 = columns(weight_1[:, at : at + ROWS])
        for half in range(2):
            net_ref[half, 2 * at : 2 * at + 2 * ROWS] = netted[
                :, half * LANES : (half + 1) * LANES
            ]
            even = net_ref[half, pl.ds(2 * at, ROWS, 2), :]
            odd = net_ref[half, pl.ds(2 * at + 1, ROWS, 2), :]
            funded = column_0 * jnp.maximum(even, 0.0) + column_1 * jnp.maximum(odd, 0.0)
            for j in range(ROWS // 16):
                block_at = at // 16 + j
                row_at = block_at // 2 * 32 + half * 16
                both_ref[block_at % 2, row_at : row_at + 16, :] = funded[j * 16 : j * 16 + 16, :]
    for out_ref, parity in ((keep_ref, core), (give_ref, 1 - core)):
        out_ref[0:HALF_ROWS, :] = both_ref[parity]


def local_sums(values, hazard, spread, trade_set):
    paths, dates, trades = values.shape
    return pl.pallas_call(
        net_kernel,
        out_shape=(HALF, HALF),
        in_specs=[ANY, ANY, ANY, ANY],
        out_specs=(VMEM, VMEM),
        scratch_shapes=[
            pltpu.VMEM(values.shape, values.dtype),
            pltpu.VMEM(hazard.shape, hazard.dtype),
            pltpu.VMEM((1, dates), jnp.float32),
            pltpu.VMEM((1, trades), jnp.int32),
            pltpu.VMEM((2, paths * dates, LANES), jnp.float32),
            pltpu.VMEM((trades, SETS), jnp.bfloat16),
            pltpu.VMEM((2, HALF_ROWS, LANES), jnp.float32),
            pltpu.VMEM((paths, LANES), jnp.float32),
            pltpu.SemaphoreType.DMA((5,)),
        ],
        compiler_params=pltpu.CompilerParams(vmem_limit_bytes=16 * MIB),
        cost_estimate=pl.CostEstimate(
            flops=2 * paths * dates * trades * SETS, bytes_accessed=5 * MIB, transcendentals=1024
        ),
        name="local_sums",
    )(in_hbm(values), in_hbm(hazard), in_hbm(spread[None, :]), in_hbm(trade_set[None, :]))


def pack_kernel(keep_ref, got_ref, out_ref, turned_ref):
    rows_ref = out_ref.reshape(XY * MESSAGE, LANES)
    core = lax.axis_index("c")
    for part in range(2):
        halves = [[], []]
        for i in range(part * 8, part * 8 + 8):
            for half in range(2):
                rows = slice(i * 32 + half * 16, i * 32 + half * 16 + 16)
                both = keep_ref[rows, :] + got_ref[rows, :]
                rows_ref[(XY - 1 - i) * MESSAGE + half * 16 : (XY - 1 - i) * MESSAGE + half * 16 + 16, :] = both
                halves[half].append(both)
        for half in range(2):
            turned_ref[part, half * LANES : (half + 1) * LANES, :] = jnp.transpose(
                jnp.concatenate(halves[half], axis=0)
            )
        row = slice(HALF_ROWS + part * 4, HALF_ROWS + part * 4 + 1)
        own, other = keep_ref[row, :], got_ref[row, :]
        first = jnp.where(core == 0, own, other)
        for i in range(XY):
            rows_ref[(XY - 1 - i) * MESSAGE + 64 + part : (XY - 1 - i) * MESSAGE + 65 + part, :] = first
            rows_ref[(XY - 1 - i) * MESSAGE + 66 + part : (XY - 1 - i) * MESSAGE + 67 + part, :] = own + other
            for owner in range(2):
                at = (XY - 1 - i) * MESSAGE + 32 + part * 16 + owner * 8
                rows_ref[at : at + 8, :] = turned_ref[part, pl.ds(2 * i + owner, 8, 32), :]


def packed(keep, got):
    return pl.pallas_call(
        pack_kernel,
        out_shape=jax.ShapeDtypeStruct((XY, MESSAGE // 2, 2, LANES), jnp.float32),
        in_specs=[VMEM, VMEM],
        out_specs=VMEM,
        scratch_shapes=[pltpu.VMEM((2, SETS, LANES), jnp.float32)],
        compiler_params=pltpu.CompilerParams(vmem_limit_bytes=4 * MIB),
        cost_estimate=pl.CostEstimate(flops=10**6, bytes_accessed=MIB, transcendentals=0),
        name="packed",
    )(keep, got)


def set_kernel(arrived_ref, earlier_ref, parts_ref):
    rows_ref = arrived_ref.reshape(XY * MESSAGE, LANES)
    prefix = jnp.zeros((2, LANES), jnp.float32)
    total = [jnp.zeros((16, LANES), jnp.float32)] * 2
    for k in range(XY):
        at = (XY - 1 - k) * MESSAGE + 64
        earlier = jnp.exp(-(prefix + rows_ref[at : at + 2, :])) * (1.0 / DATES)
        prefix = prefix + rows_ref[at + 2 : at + 4, :]
        for part in range(2):
            row = earlier[part : part + 1, :]
            earlier_ref[part, k : k + 1, :] = row
            at = (XY - 1 - k) * MESSAGE + 32 + part * 16
            total[part] = total[part] + row * rows_ref[at : at + 16, :]
    sums = jnp.sum(total[0] + total[1], axis=1, keepdims=True) * (1.0 / PATHS)
    sums = jnp.broadcast_to(sums, (16, LANES))
    order = [sums[4:8], sums[0:4], sums[12:16], sums[8:12]]
    parts_ref[...] = jnp.concatenate(order, axis=0)[:, None, :]


def set_parts(arrived):
    return pl.pallas_call(
        set_kernel,
        out_shape=(
            jax.ShapeDtypeStruct((2, XY, LANES), jnp.float32),
            jax.ShapeDtypeStruct((16, 1, LANES), jnp.float32),
        ),
        in_specs=[VMEM],
        out_specs=(VMEM, VMEM),
        compiler_params=pltpu.CompilerParams(vmem_limit_bytes=2 * MIB),
        cost_estimate=pl.CostEstimate(flops=10**6, bytes_accessed=2**19, transcendentals=4096),
        name="set_parts",
    )(arrived)


def last_kernel(arrived_ref, earlier_ref, parts_ref, paths_ref, set_ref, turned_ref):
    rows_ref = arrived_ref.reshape(XY * MESSAGE, LANES)
    chip = lax.axis_index("x") * 4 + lax.axis_index("y")
    padding = jnp.zeros((LANES - XY, LANES), jnp.float32)
    for part in range(2):
        turned_ref[part * LANES : (part + 1) * LANES, :] = jnp.transpose(
            jnp.concatenate([earlier_ref[part], padding], axis=0)
        )
    own = turned_ref[pl.ds(pl.multiple_of(chip * 16, 16), 16), :]
    total = [jnp.zeros((16, LANES), jnp.float32)] * 2
    for k in range(XY):
        weight = own[:, k : k + 1]
        for half in range(2):
            at = (XY - 1 - k) * MESSAGE + half * 16
            total[half] = total[half] + weight * rows_ref[at : at + 16, :]
    for half in range(2):
        paths_ref[:, half * LANES : (half + 1) * LANES] = total[half]
    set_ref[...] = jnp.sum(parts_ref[...], axis=0)


def last_sums(arrived, earlier, parts):
    return pl.pallas_call(
        last_kernel,
        out_shape=(
            jax.ShapeDtypeStruct((16, SETS), jnp.float32),
            jax.ShapeDtypeStruct((1, LANES), jnp.float32),
        ),
        in_specs=[VMEM, VMEM, VMEM],
        out_specs=(VMEM, VMEM),
        scratch_shapes=[pltpu.VMEM((2 * LANES, LANES), jnp.float32)],
        compiler_params=pltpu.CompilerParams(vmem_limit_bytes=2 * MIB),
        cost_estimate=pl.CostEstimate(flops=10**6, bytes_accessed=2**19, transcendentals=0),
        name="last_sums",
    )(arrived, earlier, parts)


def on_device(values, hazard, spread, trade_set):
    keep, give = local_sums(values, hazard, spread, trade_set)
    got = lax.ppermute(give, "c", [(0, 1), (1, 0)])
    chips = list(reversed(range(XY)))
    arrived = lax.all_to_all(
        packed(keep, got), ("x", "y"), 0, 0, tiled=True, axis_index_groups=[chips]
    )
    earlier, parts = set_parts(arrived)
    order = [core * 8 + (z + 4) % 8 for core in range(2) for z in range(8)]
    parts = lax.all_to_all(parts, ("c", "z"), 0, 0, tiled=True, axis_index_groups=[order])
    pathwise, sets = last_sums(arrived, earlier, parts)
    return pathwise, sets[0, 0:1]


def solution(mesh):
    split = Mesh(mesh.devices.reshape(mesh.shape["path"], 4, 4, 2), ("z", "x", "y", "c"))
    tm = ("x", "y", "c")
    every = ("z", "x", "y", "c")
    return jax.shard_map(
        on_device,
        mesh=split,
        in_specs=(P("z", tm, None), P(tm, "z"), P(tm), P()),
        out_specs=(P(every, None), P(every)),
        check_vma=False,
    )
```

```python
import jax
import jax.numpy as jnp
from jax import lax
from jax.experimental import pallas as pl
from jax.experimental.pallas import tpu as pltpu
from jax.sharding import Mesh
from jax.sharding import PartitionSpec as P

SETS = 256
LANES = 128
ROWS = 128
XY = 16
DATES = 64
PATHS = 4096
MESSAGE = 68
FAR = 10
MIB = 2**20
VMEM = pl.BlockSpec(memory_space=pltpu.VMEM)
ANY = pl.BlockSpec(memory_space=pl.ANY)
HALF_ROWS = XY * 32
HALF = jax.ShapeDtypeStruct((HALF_ROWS + 8, LANES), jnp.float32)


def columns(row):
    return jnp.transpose(jnp.broadcast_to(row, (LANES, LANES)))


def in_hbm(array):
    return pltpu.with_memory_space_constraint(array, pltpu.HBM)


def net_kernel(
    values_hbm,
    hazard_hbm,
    spread_hbm,
    set_hbm,
    keep_ref,
    give_ref,
    values_ref,
    hazard_ref,
    spread_ref,
    set_ref,
    net_ref,
    hot_ref,
    both_ref,
    own_ref,
    sem,
):
    half_paths = values_hbm.shape[0] // 2
    small = [
        pltpu.make_async_copy(set_hbm, set_ref, sem.at[0]),
        pltpu.make_async_copy(hazard_hbm, hazard_ref, sem.at[1]),
        pltpu.make_async_copy(spread_hbm, spread_ref, sem.at[2]),
    ]
    large = [
        pltpu.make_async_copy(
            values_hbm.at[pl.ds(part * half_paths, half_paths)],
            values_ref.at[pl.ds(part * half_paths, half_paths)],
            sem.at[3 + part],
        )
        for part in range(2)
    ]
    for copy in small + large:
        copy.start()
    for copy in small:
        copy.wait()
    lane = lax.broadcasted_iota(jnp.int32, (LANES, LANES), 1)
    for at in range(0, set_ref.shape[1], LANES):
        ids = columns(set_ref[:, at : at + LANES])
        for half in range(2):
            hot_ref[at : at + LANES, half * LANES : (half + 1) * LANES] = jnp.where(
                ids == lane + half * LANES, 1.0, 0.0
            ).astype(jnp.bfloat16)
    core = lax.axis_index("c")
    own = hazard_ref[0:1, :] + hazard_ref[1:2, :]
    before = jnp.where(core == 0, 0.0, own)
    weight_0 = spread_ref[:, 0:1] * jnp.exp(hazard_ref[1:2, :] - before)
    weight_1 = jnp.broadcast_to(spread_ref[:, 1:2], own.shape) * jnp.exp(-before)
    for at in range(0, own.shape[1], LANES):
        own_ref[at : at + LANES, :] = columns(own[:, at : at + LANES])
    for out_ref, parity in ((keep_ref, core), (give_ref, 1 - core)):
        for part in range(2):
            kept = [
                own_ref[pl.ds(pl.multiple_of((2 * i + parity) * 16, 16), 16), :]
                for i in range(part * 8, part * 8 + 8)
            ]
            row = jnp.transpose(jnp.concatenate(kept, axis=0))[0:1, :]
            out_ref[HALF_ROWS + part * 4 : HALF_ROWS + part * 4 + 4, :] = jnp.broadcast_to(
                row, (4, LANES)
            )
    for at in range(0, values_ref.shape[0], ROWS):
        if at % half_paths == 0:
            large[at // half_paths].wait()
        block = values_ref[at : at + ROWS].reshape(2 * ROWS, values_ref.shape[2])
        netted = jnp.dot(block, hot_ref[...], preferred_element_type=jnp.float32)
        column_0 = columns(weight_0[:, at : at + ROWS])
        column_1 = columns(weight_1[:, at : at + ROWS])
        for half in range(2):
            net_ref[half, 2 * at : 2 * at + 2 * ROWS] = netted[
                :, half * LANES : (half + 1) * LANES
            ]
            even = net_ref[half, pl.ds(2 * at, ROWS, 2), :]
            odd = net_ref[half, pl.ds(2 * at + 1, ROWS, 2), :]
            funded = column_0 * jnp.maximum(even, 0.0) + column_1 * jnp.maximum(odd, 0.0)
            for j in range(ROWS // 16):
                block_at = at // 16 + j
                row_at = block_at // 2 * 32 + half * 16
                both_ref[block_at % 2, row_at : row_at + 16, :] = funded[j * 16 : j * 16 + 16, :]
    for out_ref, parity in ((keep_ref, core), (give_ref, 1 - core)):
        out_ref[0:HALF_ROWS, :] = both_ref[parity]


def local_sums(values, hazard, spread, trade_set):
    paths, dates, trades = values.shape
    return pl.pallas_call(
        net_kernel,
        out_shape=(HALF, HALF),
        in_specs=[ANY, ANY, ANY, ANY],
        out_specs=(VMEM, VMEM),
        scratch_shapes=[
            pltpu.VMEM(values.shape, values.dtype),
            pltpu.VMEM(hazard.shape, hazard.dtype),
            pltpu.VMEM((1, dates), jnp.float32),
            pltpu.VMEM((1, trades), jnp.int32),
            pltpu.VMEM((2, paths * dates, LANES), jnp.float32),
            pltpu.VMEM((trades, SETS), jnp.bfloat16),
            pltpu.VMEM((2, HALF_ROWS, LANES), jnp.float32),
            pltpu.VMEM((paths, LANES), jnp.float32),
            pltpu.SemaphoreType.DMA((5,)),
        ],
        compiler_params=pltpu.CompilerParams(vmem_limit_bytes=16 * MIB),
        cost_estimate=pl.CostEstimate(
            flops=2 * paths * dates * trades * SETS, bytes_accessed=5 * MIB, transcendentals=1024
        ),
        name="local_sums",
    )(in_hbm(values), in_hbm(hazard), in_hbm(spread[None, :]), in_hbm(trade_set[None, :]))


def pack_kernel(keep_ref, got_ref, out_ref, turned_ref):
    rows_ref = out_ref.reshape(XY * MESSAGE, LANES)
    core = lax.axis_index("c")
    for part in range(2):
        halves = [[], []]
        for i in range(part * 8, part * 8 + 8):
            for half in range(2):
                rows = slice(i * 32 + half * 16, i * 32 + half * 16 + 16)
                both = keep_ref[rows, :] + got_ref[rows, :]
                rows_ref[(i ^ FAR) * MESSAGE + half * 16 : (i ^ FAR) * MESSAGE + half * 16 + 16, :] = both
                halves[half].append(both)
        for half in range(2):
            turned_ref[part, half * LANES : (half + 1) * LANES, :] = jnp.transpose(
                jnp.concatenate(halves[half], axis=0)
            )
        row = slice(HALF_ROWS + part * 4, HALF_ROWS + part * 4 + 1)
        own, other = keep_ref[row, :], got_ref[row, :]
        first = jnp.where(core == 0, own, other)
        for i in range(XY):
            rows_ref[(i ^ FAR) * MESSAGE + 64 + part : (i ^ FAR) * MESSAGE + 65 + part, :] = first
            rows_ref[(i ^ FAR) * MESSAGE + 66 + part : (i ^ FAR) * MESSAGE + 67 + part, :] = own + other
            for owner in range(2):
                at = (i ^ FAR) * MESSAGE + 32 + part * 16 + owner * 8
                rows_ref[at : at + 8, :] = turned_ref[part, pl.ds(2 * i + owner, 8, 32), :]


def packed(keep, got):
    return pl.pallas_call(
        pack_kernel,
        out_shape=jax.ShapeDtypeStruct((XY, MESSAGE // 2, 2, LANES), jnp.float32),
        in_specs=[VMEM, VMEM],
        out_specs=VMEM,
        scratch_shapes=[pltpu.VMEM((2, SETS, LANES), jnp.float32)],
        compiler_params=pltpu.CompilerParams(vmem_limit_bytes=4 * MIB),
        cost_estimate=pl.CostEstimate(flops=10**6, bytes_accessed=MIB, transcendentals=0),
        name="packed",
    )(keep, got)


def set_kernel(arrived_ref, earlier_ref, parts_ref):
    rows_ref = arrived_ref.reshape(XY * MESSAGE, LANES)
    prefix = jnp.zeros((2, LANES), jnp.float32)
    total = [jnp.zeros((16, LANES), jnp.float32)] * 2
    for k in range(XY):
        at = (k ^ FAR) * MESSAGE + 64
        earlier = jnp.exp(-(prefix + rows_ref[at : at + 2, :])) * (1.0 / DATES)
        prefix = prefix + rows_ref[at + 2 : at + 4, :]
        for part in range(2):
            row = earlier[part : part + 1, :]
            earlier_ref[part, k : k + 1, :] = row
            at = (k ^ FAR) * MESSAGE + 32 + part * 16
            total[part] = total[part] + row * rows_ref[at : at + 16, :]
    sums = jnp.sum(total[0] + total[1], axis=1, keepdims=True) * (1.0 / PATHS)
    sums = jnp.broadcast_to(sums, (16, LANES))
    order = [sums[4:8], sums[0:4], sums[12:16], sums[8:12]]
    parts_ref[...] = jnp.concatenate(order, axis=0)[:, None, :]


def set_parts(arrived):
    return pl.pallas_call(
        set_kernel,
        out_shape=(
            jax.ShapeDtypeStruct((2, XY, LANES), jnp.float32),
            jax.ShapeDtypeStruct((16, 1, LANES), jnp.float32),
        ),
        in_specs=[VMEM],
        out_specs=(VMEM, VMEM),
        compiler_params=pltpu.CompilerParams(vmem_limit_bytes=2 * MIB),
        cost_estimate=pl.CostEstimate(flops=10**6, bytes_accessed=2**19, transcendentals=4096),
        name="set_parts",
    )(arrived)


def last_kernel(arrived_ref, earlier_ref, parts_ref, paths_ref, set_ref, turned_ref):
    rows_ref = arrived_ref.reshape(XY * MESSAGE, LANES)
    chip = lax.axis_index("x") * 4 + lax.axis_index("y")
    padding = jnp.zeros((LANES - XY, LANES), jnp.float32)
    for part in range(2):
        turned_ref[part * LANES : (part + 1) * LANES, :] = jnp.transpose(
            jnp.concatenate([earlier_ref[part], padding], axis=0)
        )
    own = turned_ref[pl.ds(pl.multiple_of(chip * 16, 16), 16), :]
    total = [jnp.zeros((16, LANES), jnp.float32)] * 2
    for k in range(XY):
        weight = own[:, k : k + 1]
        for half in range(2):
            at = (k ^ FAR) * MESSAGE + half * 16
            total[half] = total[half] + weight * rows_ref[at : at + 16, :]
    for half in range(2):
        paths_ref[:, half * LANES : (half + 1) * LANES] = total[half]
    set_ref[...] = jnp.sum(parts_ref[...], axis=0)


def last_sums(arrived, earlier, parts):
    return pl.pallas_call(
        last_kernel,
        out_shape=(
            jax.ShapeDtypeStruct((16, SETS), jnp.float32),
            jax.ShapeDtypeStruct((1, LANES), jnp.float32),
        ),
        in_specs=[VMEM, VMEM, VMEM],
        out_specs=(VMEM, VMEM),
        scratch_shapes=[pltpu.VMEM((2 * LANES, LANES), jnp.float32)],
        compiler_params=pltpu.CompilerParams(vmem_limit_bytes=2 * MIB),
        cost_estimate=pl.CostEstimate(flops=10**6, bytes_accessed=2**19, transcendentals=0),
        name="last_sums",
    )(arrived, earlier, parts)


def on_device(values, hazard, spread, trade_set):
    keep, give = local_sums(values, hazard, spread, trade_set)
    got = lax.ppermute(give, "c", [(0, 1), (1, 0)])
    chips = [i ^ FAR for i in range(XY)]
    arrived = lax.all_to_all(
        packed(keep, got), ("x", "y"), 0, 0, tiled=True, axis_index_groups=[chips]
    )
    earlier, parts = set_parts(arrived)
    order = [core * 8 + (z + 4) % 8 for core in range(2) for z in range(8)]
    parts = lax.all_to_all(parts, ("c", "z"), 0, 0, tiled=True, axis_index_groups=[order])
    pathwise, sets = last_sums(arrived, earlier, parts)
    return pathwise, sets[0, 0:1]


def solution(mesh):
    split = Mesh(mesh.devices.reshape(mesh.shape["path"], 4, 4, 2), ("z", "x", "y", "c"))
    tm = ("x", "y", "c")
    every = ("z", "x", "y", "c")
    return jax.shard_map(
        on_device,
        mesh=split,
        in_specs=(P("z", tm, None), P(tm, "z"), P(tm), P()),
        out_specs=(P(every, None), P(every)),
        check_vma=False,
    )
```

```python
import jax
import jax.numpy as jnp
from jax import lax
from jax.experimental import pallas as pl
from jax.experimental.pallas import tpu as pltpu
from jax.sharding import Mesh
from jax.sharding import PartitionSpec as P

SETS = 256
LANES = 128
ROWS = 128
XY = 16
DATES = 64
PATHS = 4096
MESSAGE = 68
FAR = 10
MIB = 2**20
VMEM = pl.BlockSpec(memory_space=pltpu.VMEM)
ANY = pl.BlockSpec(memory_space=pl.ANY)
HALF_ROWS = XY * 32
HALF = jax.ShapeDtypeStruct((HALF_ROWS + 8, LANES), jnp.float32)


def columns(row):
    return jnp.transpose(jnp.broadcast_to(row, (LANES, LANES)))


def in_hbm(array):
    return pltpu.with_memory_space_constraint(array, pltpu.HBM)


def net_kernel(
    values_hbm,
    hazard_hbm,
    spread_hbm,
    set_hbm,
    keep_ref,
    give_ref,
    values_ref,
    hazard_ref,
    spread_ref,
    set_ref,
    net_ref,
    hot_ref,
    both_ref,
    own_ref,
    sem,
):
    half_paths = values_hbm.shape[0] // 2
    small = [
        pltpu.make_async_copy(set_hbm, set_ref, sem.at[0]),
        pltpu.make_async_copy(hazard_hbm, hazard_ref, sem.at[1]),
        pltpu.make_async_copy(spread_hbm, spread_ref, sem.at[2]),
    ]
    large = [
        pltpu.make_async_copy(
            values_hbm.at[pl.ds(part * half_paths, half_paths)],
            values_ref.at[pl.ds(part * half_paths, half_paths)],
            sem.at[3 + part],
        )
        for part in range(2)
    ]
    for copy in small + large:
        copy.start()
    for copy in small:
        copy.wait()
    lane = lax.broadcasted_iota(jnp.int32, (LANES, LANES), 1)
    for at in range(0, set_ref.shape[1], LANES):
        ids = columns(set_ref[:, at : at + LANES])
        for half in range(2):
            hot_ref[at : at + LANES, half * LANES : (half + 1) * LANES] = jnp.where(
                ids == lane + half * LANES, 1.0, 0.0
            ).astype(jnp.bfloat16)
    core = lax.axis_index("c")
    own = hazard_ref[0:1, :] + hazard_ref[1:2, :]
    before = jnp.where(core == 0, 0.0, own)
    weight_0 = spread_ref[:, 0:1] * jnp.exp(hazard_ref[1:2, :] - before)
    weight_1 = jnp.broadcast_to(spread_ref[:, 1:2], own.shape) * jnp.exp(-before)
    for at in range(0, own.shape[1], LANES):
        own_ref[at : at + LANES, :] = columns(own[:, at : at + LANES])
    for out_ref, parity in ((keep_ref, core), (give_ref, 1 - core)):
        for part in range(2):
            kept = [
                own_ref[pl.ds(pl.multiple_of((2 * i + parity) * 16, 16), 16), :]
                for i in range(part * 8, part * 8 + 8)
            ]
            row = jnp.transpose(jnp.concatenate(kept, axis=0))[0:1, :]
            out_ref[HALF_ROWS + part * 4 : HALF_ROWS + part * 4 + 4, :] = jnp.broadcast_to(
                row, (4, LANES)
            )
    for at in range(0, values_ref.shape[0], ROWS):
        if at % half_paths == 0:
            large[at // half_paths].wait()
        block = values_ref[at : at + ROWS].reshape(2 * ROWS, values_ref.shape[2])
        netted = jnp.dot(block, hot_ref[...], preferred_element_type=jnp.float32)
        column_0 = columns(weight_0[:, at : at + ROWS])
        column_1 = columns(weight_1[:, at : at + ROWS])
        for half in range(2):
            net_ref[half, 2 * at : 2 * at + 2 * ROWS] = netted[
                :, half * LANES : (half + 1) * LANES
            ]
            even = net_ref[half, pl.ds(2 * at, ROWS, 2), :]
            odd = net_ref[half, pl.ds(2 * at + 1, ROWS, 2), :]
            funded = column_0 * jnp.maximum(even, 0.0) + column_1 * jnp.maximum(odd, 0.0)
            for j in range(ROWS // 16):
                block_at = at // 16 + j
                row_at = block_at // 2 * 32 + half * 16
                both_ref[block_at % 2, row_at : row_at + 16, :] = funded[j * 16 : j * 16 + 16, :]
    for out_ref, parity in ((keep_ref, core), (give_ref, 1 - core)):
        out_ref[0:HALF_ROWS, :] = both_ref[parity]


def local_sums(values, hazard, spread, trade_set):
    paths, dates, trades = values.shape
    return pl.pallas_call(
        net_kernel,
        out_shape=(HALF, HALF),
        in_specs=[ANY, ANY, ANY, ANY],
        out_specs=(VMEM, VMEM),
        scratch_shapes=[
            pltpu.VMEM(values.shape, values.dtype),
            pltpu.VMEM(hazard.shape, hazard.dtype),
            pltpu.VMEM((1, dates), jnp.float32),
            pltpu.VMEM((1, trades), jnp.int32),
            pltpu.VMEM((2, paths * dates + 8, LANES), jnp.float32),
            pltpu.VMEM((trades, SETS), jnp.bfloat16),
            pltpu.VMEM((2, HALF_ROWS, LANES), jnp.float32),
            pltpu.VMEM((paths, LANES), jnp.float32),
            pltpu.SemaphoreType.DMA((5,)),
        ],
        compiler_params=pltpu.CompilerParams(vmem_limit_bytes=16 * MIB),
        cost_estimate=pl.CostEstimate(
            flops=2 * paths * dates * trades * SETS, bytes_accessed=5 * MIB, transcendentals=1024
        ),
        name="local_sums",
    )(in_hbm(values), in_hbm(hazard), in_hbm(spread[None, :]), in_hbm(trade_set[None, :]))


def pack_kernel(keep_ref, got_ref, out_ref, turned_ref):
    rows_ref = out_ref.reshape(XY * MESSAGE, LANES)
    core = lax.axis_index("c")
    for part in range(2):
        halves = [[], []]
        for i in range(part * 8, part * 8 + 8):
            for half in range(2):
                rows = slice(i * 32 + half * 16, i * 32 + half * 16 + 16)
                both = keep_ref[rows, :] + got_ref[rows, :]
                rows_ref[(i ^ FAR) * MESSAGE + half * 16 : (i ^ FAR) * MESSAGE + half * 16 + 16, :] = both
                halves[half].append(both)
        for half in range(2):
            turned_ref[part, half * LANES : (half + 1) * LANES, :] = jnp.transpose(
                jnp.concatenate(halves[half], axis=0)
            )
        row = slice(HALF_ROWS + part * 4, HALF_ROWS + part * 4 + 1)
        own, other = keep_ref[row, :], got_ref[row, :]
        first = jnp.where(core == 0, own, other)
        for i in range(XY):
            rows_ref[(i ^ FAR) * MESSAGE + 64 + part : (i ^ FAR) * MESSAGE + 65 + part, :] = first
            rows_ref[(i ^ FAR) * MESSAGE + 66 + part : (i ^ FAR) * MESSAGE + 67 + part, :] = own + other
            for owner in range(2):
                at = (i ^ FAR) * MESSAGE + 32 + part * 16 + owner * 8
                rows_ref[at : at + 8, :] = turned_ref[part, pl.ds(2 * i + owner, 8, 32), :]


def packed(keep, got):
    return pl.pallas_call(
        pack_kernel,
        out_shape=jax.ShapeDtypeStruct((XY, MESSAGE // 2, 2, LANES), jnp.float32),
        in_specs=[VMEM, VMEM],
        out_specs=VMEM,
        scratch_shapes=[pltpu.VMEM((2, SETS + 32, LANES), jnp.float32)],
        compiler_params=pltpu.CompilerParams(vmem_limit_bytes=4 * MIB),
        cost_estimate=pl.CostEstimate(flops=10**6, bytes_accessed=MIB, transcendentals=0),
        name="packed",
    )(keep, got)


def set_kernel(arrived_ref, earlier_ref, parts_ref):
    rows_ref = arrived_ref.reshape(XY * MESSAGE, LANES)
    prefix = jnp.zeros((2, LANES), jnp.float32)
    total = [jnp.zeros((16, LANES), jnp.float32)] * 2
    for k in range(XY):
        at = (k ^ FAR) * MESSAGE + 64
        earlier = jnp.exp(-(prefix + rows_ref[at : at + 2, :])) * (1.0 / DATES)
        prefix = prefix + rows_ref[at + 2 : at + 4, :]
        for part in range(2):
            row = earlier[part : part + 1, :]
            earlier_ref[part, k : k + 1, :] = row
            at = (k ^ FAR) * MESSAGE + 32 + part * 16
            total[part] = total[part] + row * rows_ref[at : at + 16, :]
    sums = jnp.sum(total[0] + total[1], axis=1, keepdims=True) * (1.0 / PATHS)
    sums = jnp.broadcast_to(sums, (16, LANES))
    order = [sums[4:8], sums[0:4], sums[12:16], sums[8:12]]
    parts_ref[...] = jnp.concatenate(order, axis=0)[:, None, :]


def set_parts(arrived):
    return pl.pallas_call(
        set_kernel,
        out_shape=(
            jax.ShapeDtypeStruct((2, XY, LANES), jnp.float32),
            jax.ShapeDtypeStruct((16, 1, LANES), jnp.float32),
        ),
        in_specs=[VMEM],
        out_specs=(VMEM, VMEM),
        compiler_params=pltpu.CompilerParams(vmem_limit_bytes=2 * MIB),
        cost_estimate=pl.CostEstimate(flops=10**6, bytes_accessed=2**19, transcendentals=4096),
        name="set_parts",
    )(arrived)


def last_kernel(arrived_ref, earlier_ref, parts_ref, paths_ref, set_ref, turned_ref):
    rows_ref = arrived_ref.reshape(XY * MESSAGE, LANES)
    chip = lax.axis_index("x") * 4 + lax.axis_index("y")
    padding = jnp.zeros((LANES - XY, LANES), jnp.float32)
    for part in range(2):
        turned_ref[part * LANES : (part + 1) * LANES, :] = jnp.transpose(
            jnp.concatenate([earlier_ref[part], padding], axis=0)
        )
    own = turned_ref[pl.ds(pl.multiple_of(chip * 16, 16), 16), :]
    total = [jnp.zeros((16, LANES), jnp.float32)] * 2
    for k in range(XY):
        weight = own[:, k : k + 1]
        for half in range(2):
            at = (k ^ FAR) * MESSAGE + half * 16
            total[half] = total[half] + weight * rows_ref[at : at + 16, :]
    for half in range(2):
        paths_ref[:, half * LANES : (half + 1) * LANES] = total[half]
    set_ref[...] = jnp.sum(parts_ref[...], axis=0)


def last_sums(arrived, earlier, parts):
    return pl.pallas_call(
        last_kernel,
        out_shape=(
            jax.ShapeDtypeStruct((16, SETS), jnp.float32),
            jax.ShapeDtypeStruct((1, LANES), jnp.float32),
        ),
        in_specs=[VMEM, VMEM, VMEM],
        out_specs=(VMEM, VMEM),
        scratch_shapes=[pltpu.VMEM((2 * LANES, LANES), jnp.float32)],
        compiler_params=pltpu.CompilerParams(vmem_limit_bytes=2 * MIB),
        cost_estimate=pl.CostEstimate(flops=10**6, bytes_accessed=2**19, transcendentals=0),
        name="last_sums",
    )(arrived, earlier, parts)


def on_device(values, hazard, spread, trade_set):
    keep, give = local_sums(values, hazard, spread, trade_set)
    got = lax.ppermute(give, "c", [(0, 1), (1, 0)])
    chips = [i ^ FAR for i in range(XY)]
    arrived = lax.all_to_all(
        packed(keep, got), ("x", "y"), 0, 0, tiled=True, axis_index_groups=[chips]
    )
    earlier, parts = set_parts(arrived)
    order = [core * 8 + (z + 4) % 8 for core in range(2) for z in range(8)]
    parts = lax.all_to_all(parts, ("c", "z"), 0, 0, tiled=True, axis_index_groups=[order])
    pathwise, sets = last_sums(arrived, earlier, parts)
    return pathwise, sets[0, 0:1]


def solution(mesh):
    split = Mesh(mesh.devices.reshape(mesh.shape["path"], 4, 4, 2), ("z", "x", "y", "c"))
    tm = ("x", "y", "c")
    every = ("z", "x", "y", "c")
    return jax.shard_map(
        on_device,
        mesh=split,
        in_specs=(P("z", tm, None), P(tm, "z"), P(tm), P()),
        out_specs=(P(every, None), P(every)),
        check_vma=False,
    )
```

```python
import jax
import jax.numpy as jnp
from jax import lax
from jax.experimental import pallas as pl
from jax.experimental.pallas import tpu as pltpu
from jax.sharding import Mesh
from jax.sharding import PartitionSpec as P

SETS = 256
LANES = 128
ROWS = 128
XY = 16
DATES = 64
PATHS = 4096
MESSAGE = 68
FAR = 10
MIB = 2**20
VMEM = pl.BlockSpec(memory_space=pltpu.VMEM)
ANY = pl.BlockSpec(memory_space=pl.ANY)
HALF_ROWS = XY * 32
HALF = jax.ShapeDtypeStruct((HALF_ROWS + 8, LANES), jnp.float32)


def columns(row):
    return jnp.transpose(jnp.broadcast_to(row, (LANES, LANES)))


def in_hbm(array):
    return pltpu.with_memory_space_constraint(array, pltpu.HBM)


def net_kernel(
    values_hbm,
    hazard_hbm,
    spread_hbm,
    set_hbm,
    keep_ref,
    give_ref,
    values_ref,
    hazard_ref,
    spread_ref,
    set_ref,
    net_ref,
    hot_ref,
    both_ref,
    own_ref,
    sem,
):
    half_paths = values_hbm.shape[0] // 2
    small = [
        pltpu.make_async_copy(set_hbm, set_ref, sem.at[0]),
        pltpu.make_async_copy(hazard_hbm, hazard_ref, sem.at[1]),
        pltpu.make_async_copy(spread_hbm, spread_ref, sem.at[2]),
    ]
    large = [
        pltpu.make_async_copy(
            values_hbm.at[pl.ds(part * half_paths, half_paths)],
            values_ref.at[pl.ds(part * half_paths, half_paths)],
            sem.at[3 + part],
        )
        for part in range(2)
    ]
    for copy in small + large:
        copy.start()
    for copy in small:
        copy.wait()
    lane = lax.broadcasted_iota(jnp.int32, (LANES, LANES), 1)
    for at in range(0, set_ref.shape[1], LANES):
        ids = columns(set_ref[:, at : at + LANES])
        for half in range(2):
            hot_ref[at : at + LANES, half * LANES : (half + 1) * LANES] = jnp.where(
                ids == lane + half * LANES, 1.0, 0.0
            ).astype(jnp.bfloat16)
    core = lax.axis_index("c")
    own = hazard_ref[0:1, :] + hazard_ref[1:2, :]
    before = jnp.where(core == 0, 0.0, own)
    weight_0 = spread_ref[:, 0:1] * jnp.exp(hazard_ref[1:2, :] - before)
    weight_1 = jnp.broadcast_to(spread_ref[:, 1:2], own.shape) * jnp.exp(-before)
    for at in range(0, own.shape[1], LANES):
        own_ref[at : at + LANES, :] = columns(own[:, at : at + LANES])
    for out_ref, parity in ((keep_ref, core), (give_ref, 1 - core)):
        for part in range(2):
            kept = [
                own_ref[pl.ds(pl.multiple_of((2 * i + parity) * 16, 16), 16), :]
                for i in range(part * 8, part * 8 + 8)
            ]
            row = jnp.transpose(jnp.concatenate(kept, axis=0))[0:1, :]
            out_ref[HALF_ROWS + part * 4 : HALF_ROWS + part * 4 + 4, :] = jnp.broadcast_to(
                row, (4, LANES)
            )
    for at in range(0, values_ref.shape[0], ROWS):
        if at % half_paths == 0:
            large[at // half_paths].wait()
        block = values_ref[at : at + ROWS].reshape(2 * ROWS, values_ref.shape[2])
        netted = jnp.dot(block, hot_ref[...], preferred_element_type=jnp.float32)
        column_0 = columns(weight_0[:, at : at + ROWS])
        column_1 = columns(weight_1[:, at : at + ROWS])
        for half in range(2):
            net_ref[half, 2 * at : 2 * at + 2 * ROWS] = netted[
                :, half * LANES : (half + 1) * LANES
            ]
            even = net_ref[half, pl.ds(2 * at, ROWS, 2), :]
            odd = net_ref[half, pl.ds(2 * at + 1, ROWS, 2), :]
            funded = column_0 * jnp.maximum(even, 0.0) + column_1 * jnp.maximum(odd, 0.0)
            for j in range(ROWS // 16):
                block_at = at // 16 + j
                row_at = block_at // 2 * 32 + half * 16
                both_ref[block_at % 2, row_at : row_at + 16, :] = funded[j * 16 : j * 16 + 16, :]
    for out_ref, parity in ((keep_ref, core), (give_ref, 1 - core)):
        out_ref[0:HALF_ROWS, :] = both_ref[parity]


def local_sums(values, hazard, spread, trade_set):
    paths, dates, trades = values.shape
    return pl.pallas_call(
        net_kernel,
        out_shape=(HALF, HALF),
        in_specs=[ANY, ANY, ANY, ANY],
        out_specs=(VMEM, VMEM),
        scratch_shapes=[
            pltpu.VMEM(values.shape, values.dtype),
            pltpu.VMEM(hazard.shape, hazard.dtype),
            pltpu.VMEM((1, dates), jnp.float32),
            pltpu.VMEM((1, trades), jnp.int32),
            pltpu.VMEM((2, paths * dates + 8, LANES), jnp.float32),
            pltpu.VMEM((trades, SETS), jnp.bfloat16),
            pltpu.VMEM((2, HALF_ROWS, LANES), jnp.float32),
            pltpu.VMEM((paths, LANES), jnp.float32),
            pltpu.SemaphoreType.DMA((5,)),
        ],
        compiler_params=pltpu.CompilerParams(vmem_limit_bytes=16 * MIB),
        cost_estimate=pl.CostEstimate(
            flops=2 * paths * dates * trades * SETS, bytes_accessed=5 * MIB, transcendentals=1024
        ),
        name="local_sums",
    )(in_hbm(values), in_hbm(hazard), in_hbm(spread[None, :]), in_hbm(trade_set[None, :]))


def pack_kernel(keep_ref, got_ref, out_ref, turned_ref):
    rows_ref = out_ref.reshape(XY * MESSAGE, LANES)
    core = lax.axis_index("c")
    for part in range(2):
        halves = [[], []]
        for i in range(part * 8, part * 8 + 8):
            for half in range(2):
                rows = slice(i * 32 + half * 16, i * 32 + half * 16 + 16)
                both = keep_ref[rows, :] + got_ref[rows, :]
                rows_ref[(i ^ FAR) * MESSAGE + half * 16 : (i ^ FAR) * MESSAGE + half * 16 + 16, :] = both
                halves[half].append(both)
        for half in range(2):
            turned_ref[part, half * LANES : (half + 1) * LANES, :] = jnp.transpose(
                jnp.concatenate(halves[half], axis=0)
            )
        row = slice(HALF_ROWS + part * 4, HALF_ROWS + part * 4 + 1)
        own, other = keep_ref[row, :], got_ref[row, :]
        first = jnp.where(core == 0, own, other)
        for i in range(XY):
            rows_ref[(i ^ FAR) * MESSAGE + 64 + part : (i ^ FAR) * MESSAGE + 65 + part, :] = first
            rows_ref[(i ^ FAR) * MESSAGE + 66 + part : (i ^ FAR) * MESSAGE + 67 + part, :] = own + other
            for owner in range(2):
                at = (i ^ FAR) * MESSAGE + 32 + part * 16 + owner * 8
                rows_ref[at : at + 8, :] = turned_ref[part, pl.ds(2 * i + owner, 8, 32), :]


def packed(keep, got):
    return pl.pallas_call(
        pack_kernel,
        out_shape=jax.ShapeDtypeStruct((XY, MESSAGE // 2, 2, LANES), jnp.float32),
        in_specs=[VMEM, VMEM],
        out_specs=VMEM,
        scratch_shapes=[pltpu.VMEM((2, SETS + 32, LANES), jnp.float32)],
        compiler_params=pltpu.CompilerParams(vmem_limit_bytes=4 * MIB),
        cost_estimate=pl.CostEstimate(flops=10**6, bytes_accessed=MIB, transcendentals=0),
        name="packed",
    )(keep, got)


def set_kernel(arrived_ref, earlier_ref, parts_ref):
    rows_ref = arrived_ref.reshape(XY * MESSAGE, LANES)
    prefix = jnp.zeros((2, LANES), jnp.float32)
    total = [jnp.zeros((16, LANES), jnp.float32)] * 2
    for k in range(XY):
        at = (k ^ FAR) * MESSAGE + 64
        earlier = jnp.exp(-(prefix + rows_ref[at : at + 2, :])) * (1.0 / DATES)
        prefix = prefix + rows_ref[at + 2 : at + 4, :]
        for part in range(2):
            row = earlier[part : part + 1, :]
            earlier_ref[part, k : k + 1, :] = row
            at = (k ^ FAR) * MESSAGE + 32 + part * 16
            total[part] = total[part] + row * rows_ref[at : at + 16, :]
    sums = jnp.sum(total[0] + total[1], axis=1, keepdims=True) * (1.0 / PATHS)
    sums = jnp.broadcast_to(sums, (16, LANES))
    order = [sums[5:8], sums[0:5], sums[13:16], sums[8:13]]
    parts_ref[...] = jnp.concatenate(order, axis=0)[:, None, :]


def set_parts(arrived):
    return pl.pallas_call(
        set_kernel,
        out_shape=(
            jax.ShapeDtypeStruct((2, XY, LANES), jnp.float32),
            jax.ShapeDtypeStruct((16, 1, LANES), jnp.float32),
        ),
        in_specs=[VMEM],
        out_specs=(VMEM, VMEM),
        compiler_params=pltpu.CompilerParams(vmem_limit_bytes=2 * MIB),
        cost_estimate=pl.CostEstimate(flops=10**6, bytes_accessed=2**19, transcendentals=4096),
        name="set_parts",
    )(arrived)


def last_kernel(arrived_ref, earlier_ref, parts_ref, paths_ref, set_ref, turned_ref):
    rows_ref = arrived_ref.reshape(XY * MESSAGE, LANES)
    chip = lax.axis_index("x") * 4 + lax.axis_index("y")
    padding = jnp.zeros((LANES - XY, LANES), jnp.float32)
    for part in range(2):
        turned_ref[part * LANES : (part + 1) * LANES, :] = jnp.transpose(
            jnp.concatenate([earlier_ref[part], padding], axis=0)
        )
    own = turned_ref[pl.ds(pl.multiple_of(chip * 16, 16), 16), :]
    total = [jnp.zeros((16, LANES), jnp.float32)] * 2
    for k in range(XY):
        weight = own[:, k : k + 1]
        for half in range(2):
            at = (k ^ FAR) * MESSAGE + half * 16
            total[half] = total[half] + weight * rows_ref[at : at + 16, :]
    for half in range(2):
        paths_ref[:, half * LANES : (half + 1) * LANES] = total[half]
    set_ref[...] = jnp.sum(parts_ref[...], axis=0)


def last_sums(arrived, earlier, parts):
    return pl.pallas_call(
        last_kernel,
        out_shape=(
            jax.ShapeDtypeStruct((16, SETS), jnp.float32),
            jax.ShapeDtypeStruct((1, LANES), jnp.float32),
        ),
        in_specs=[VMEM, VMEM, VMEM],
        out_specs=(VMEM, VMEM),
        scratch_shapes=[pltpu.VMEM((2 * LANES, LANES), jnp.float32)],
        compiler_params=pltpu.CompilerParams(vmem_limit_bytes=2 * MIB),
        cost_estimate=pl.CostEstimate(flops=10**6, bytes_accessed=2**19, transcendentals=0),
        name="last_sums",
    )(arrived, earlier, parts)


def on_device(values, hazard, spread, trade_set):
    keep, give = local_sums(values, hazard, spread, trade_set)
    got = lax.ppermute(give, "c", [(0, 1), (1, 0)])
    chips = [i ^ FAR for i in range(XY)]
    arrived = lax.all_to_all(
        packed(keep, got), ("x", "y"), 0, 0, tiled=True, axis_index_groups=[chips]
    )
    earlier, parts = set_parts(arrived)
    order = [core * 8 + (z + 5) % 8 for core in range(2) for z in range(8)]
    parts = lax.all_to_all(parts, ("c", "z"), 0, 0, tiled=True, axis_index_groups=[order])
    pathwise, sets = last_sums(arrived, earlier, parts)
    return pathwise, sets[0, 0:1]


def solution(mesh):
    split = Mesh(mesh.devices.reshape(mesh.shape["path"], 4, 4, 2), ("z", "x", "y", "c"))
    tm = ("x", "y", "c")
    every = ("z", "x", "y", "c")
    return jax.shard_map(
        on_device,
        mesh=split,
        in_specs=(P("z", tm, None), P(tm, "z"), P(tm), P()),
        out_specs=(P(every, None), P(every)),
        check_vma=False,
    )
```
